128 devices in a mesh: grp: 4 (over x_lo, core), dp: 32 (over y, x_hi, z).
Axes of the slice: x: 4 (x_hi: 2, x_lo: 2; x = x_hi * 2 + x_lo), y: 4, z: 4, core: 2. Of those that a mesh axis runs over, the one named last changes fastest.
Arguments:
- photo_vectors_raw: bfloat16 [131072, 768], P(('grp', 'dp')), may hold values from -0.21875 to 0.21875
- sentence_vectors_raw: bfloat16 [131072, 768], P(('grp', 'dp')), may hold values from -0.21875 to 0.21875
- companion_index: int32 [128, 1024], P(('grp', 'dp')), may hold values from 0 to 1023, each once within a row
- exponent_of_sharpness: float32 [1], replicated, may hold values from 1 to 2.3
- affinity_offset: float32 [1], replicated, may hold values from -4 to -1
Outputs:
- image_grad: float32 [131072, 768], P(('grp', 'dp'))
- text_grad: float32 [131072, 768], P(('grp', 'dp'))
The draws below stay inside these ranges and needn't reach their ends.
Inputs may be any that keep to these rules, and one draw needn't show every extreme that they name: Each row of companion_index is a permutation of 0 to 1023.
All inputs are finite; a program needn't handle non-finite values.
Results may differ from the reference program's by a relative error of at most 0.0055.
Values may be sent and summed in bfloat16 or wider, within the bound.
No kernel may reach another device: no remote copies, remote signals or barrier semaphores. Data moves between devices by JAX's collectives and lax.ppermute only.
A program may use at most 128 MiB of HBM per device.

```python
import jax
import jax.numpy as jnp
from jax import lax

D = 768
ROWS = 1024
SEGMENT_COUNT = 128
TOKENS = 131072


def steps_of(own_key, dims, shards, smallest, top_value):
    level = 1.0
    for position, blocks in shards:
        heights = jax.random.uniform(jax.random.fold_in(jax.random.fold_in(own_key, 6), position), (blocks,), jnp.float32, smallest / len(shards), top_value / len(shards))
        level = level * jnp.repeat(jnp.exp(heights), dims[position] // blocks).reshape((-1,) + (1,) * (len(dims) - 1 - position))
    return level


def scatter_about(stream_key, dims, deviation, limit, shards=(), kind=jnp.bfloat16):
    level = steps_of(stream_key, dims, shards, -0.22, 0.18) if shards else 1.0
    drawn = jax.random.normal(stream_key, dims, jnp.float32) * deviation * level
    return jnp.minimum(jnp.maximum(drawn, -limit), limit).astype(kind)


def setup_inputs(seed: int = 0) -> dict:
    key_list = jax.random.split(jax.random.key(seed), 6)
    return {
        "photo_vectors_raw": scatter_about(key_list[0], (TOKENS, D), D ** -0.5, 0.21875, ((0, 128),)),
        "sentence_vectors_raw": scatter_about(key_list[1], (TOKENS, D), D ** -0.5, 0.21875, ((0, 128),)),
        "companion_index": jax.vmap(lambda own: jax.random.permutation(own, ROWS))(jax.random.split(key_list[2], SEGMENT_COUNT)).reshape((SEGMENT_COUNT, ROWS)).astype(jnp.int32),
        "exponent_of_sharpness": jnp.clip(jax.random.uniform(key_list[3], (1,), jnp.float32, 1.0, 2.3), 1.0, 2.3),
        "affinity_offset": jnp.clip(jax.random.uniform(key_list[4], (1,), jnp.float32, -4.0, -1.0), -4.0, -1.0),
    }


def unit_rows(raw):
    values = raw.astype(jnp.float32)
    inverse_norm = lax.rsqrt(lax.optimization_barrier(jnp.sum(values * values, -1, keepdims=True)) + 1e-06)
    return (values * inverse_norm, inverse_norm)

def gradient_panel(picture_rows, caption_rows, matching_pairs, sharpness_factor, block_distance):
    score_matrix = sharpness_factor * jnp.dot(picture_rows, caption_rows.T, preferred_element_type=jnp.float32) + block_distance
    if matching_pairs is None:
        target_labels = -1.0
    else:
        target_labels = jnp.where(matching_pairs, 1.0, -1.0)
    return (sharpness_factor * -target_labels * jax.nn.sigmoid(-target_labels * score_matrix)).astype(jnp.bfloat16)

def unit_backward(grad, unit, inverse_norm):
    return inverse_norm * (grad - unit * lax.optimization_barrier(jnp.sum(unit * grad, -1, keepdims=True)))

def reference(photo_vectors_raw, sentence_vectors_raw, companion_index, exponent_of_sharpness, affinity_offset):
    sharpness_factor = jnp.exp(exponent_of_sharpness[0])
    block_distance = affinity_offset[0]
    image_unit, image_norm = unit_rows(photo_vectors_raw)
    text_unit, text_norm = unit_rows(sentence_vectors_raw)
    image_blocks = image_unit.astype(jnp.bfloat16).reshape(SEGMENT_COUNT, ROWS, D)
    text_blocks = text_unit.astype(jnp.bfloat16).reshape(SEGMENT_COUNT, ROWS, D)

    def per_block(items):
        picture_rows, caption_rows, preceding_block, following_block, pairing = items
        matching_pairs = pairing[:, None] == jnp.arange(ROWS, dtype=jnp.int32)[None, :]
        local_panel = gradient_panel(picture_rows, caption_rows, matching_pairs, sharpness_factor, block_distance)
        leftward_panel = gradient_panel(picture_rows, preceding_block, None, sharpness_factor, block_distance)
        rightward_panel = gradient_panel(picture_rows, following_block, None, sharpness_factor, block_distance)
        image_part = jnp.dot(local_panel, caption_rows, preferred_element_type=jnp.float32)
        image_part = image_part + jnp.dot(leftward_panel, preceding_block, preferred_element_type=jnp.float32)
        image_part = image_part + jnp.dot(rightward_panel, following_block, preferred_element_type=jnp.float32)
        text_own = jnp.dot(local_panel.T, picture_rows, preferred_element_type=jnp.float32)
        text_left = jnp.dot(leftward_panel.T, picture_rows, preferred_element_type=jnp.float32)
        text_right = jnp.dot(rightward_panel.T, picture_rows, preferred_element_type=jnp.float32)
        return (image_part, text_own, text_left, text_right)
    image_part, text_own, text_left, text_right = lax.map(per_block, (image_blocks, text_blocks, jnp.roll(text_blocks, 1, 0), jnp.roll(text_blocks, -1, 0), companion_index))
    text_part = text_own + jnp.roll(text_left, -1, 0) + jnp.roll(text_right, 1, 0)
    image_grad = unit_backward(image_part.reshape(TOKENS, D), image_unit, image_norm)
    text_grad = unit_backward(text_part.reshape(TOKENS, D), text_unit, text_norm)
    return (image_grad, text_grad)
```

```python
import functools

import jax
import jax.numpy as jnp
from jax import lax
from jax.experimental import pallas as pl
from jax.experimental.pallas import tpu as pltpu
from jax.sharding import PartitionSpec as P

AXES = ("grp", "dp")
LOG2E = 1.4426950408889634
VMEM_LIMIT = 32 * 2**20


def swapped(x, parity):
    devices = lax.axis_size(AXES)
    pairs = []
    for k in range(parity, devices, 2):
        after = (k + 1) % devices
        pairs += [(k, after), (after, k)]
    return lax.ppermute(x, AXES, pairs)


def prepare_kernel(image_ref, text_ref, image_out, image_norm_out, text_out, text_norm_out):
    for raw_ref, out_ref, norm_ref in (
        (image_ref, image_out, image_norm_out),
        (text_ref, text_out, text_norm_out),
    ):
        values = raw_ref[...].astype(jnp.float32)
        norm = lax.rsqrt(jnp.sum(values * values, -1, keepdims=True) + 1e-06)
        out_ref[...] = (values * norm).astype(jnp.bfloat16)
        norm_ref[...] = norm


def prepare(image, text, step=256):
    rows, width = image.shape
    block = pl.BlockSpec((step, width), lambda i: (i, 0))
    column = pl.BlockSpec((step, 1), lambda i: (i, 0))
    unit = jax.ShapeDtypeStruct((rows, width), jnp.bfloat16)
    norm = jax.ShapeDtypeStruct((rows, 1), jnp.float32)
    return pl.pallas_call(
        prepare_kernel,
        grid=(rows // step,),
        in_specs=[block, block],
        out_specs=[block, column, block, column],
        out_shape=[unit, norm, unit, norm],
        compiler_params=pltpu.CompilerParams(vmem_limit_bytes=VMEM_LIMIT),
        cost_estimate=pl.CostEstimate(
            flops=8 * rows * width, bytes_accessed=8 * rows * width, transcendentals=2 * rows
        ),
        name="prepare",
    )(image, text)


def side_kernel(*refs, label, raw_other, has_sum, final, chunk):
    refs = list(refs)
    scalars, own_ref, other_ref = refs[:3]
    refs = refs[3:]
    pair_ref = refs.pop(0) if label else None
    sum_ref = refs.pop(0) if has_sum else None
    raw_ref, norm_ref = (refs.pop(0), refs.pop(0)) if final else (None, None)
    out_ref = refs.pop(0)
    count = other_ref.shape[0]
    if raw_other:
        unit_ref = refs.pop(0)

        @pl.when(pl.program_id(0) == 0)
        def _():
            for r in range(0, count, 256):
                values = other_ref[r : r + 256, :].astype(jnp.float32)
                norm = lax.rsqrt(jnp.sum(values * values, -1, keepdims=True) + 1e-06)
                unit_ref[r : r + 256, :] = (values * norm).astype(jnp.bfloat16)
    else:
        unit_ref = other_ref
    slope, shift, floor = scalars[0], scalars[1], scalars[2]
    own = own_ref[...]
    rows = own.shape[0]
    if label == "row":
        row_id = pl.program_id(0) * rows + lax.broadcasted_iota(jnp.int32, (rows, chunk), 0)
    grads = []
    for c in range(0, count, chunk):
        other = unit_ref[c : c + chunk, :]
        scores = lax.dot_general(
            own, other, (((1,), (1,)), ((), ())), preferred_element_type=jnp.float32
        )
        power = slope * scores + shift
        if label:
            if label == "row":
                match = row_id == pair_ref[:, c : c + chunk]
            else:
                match = pair_ref[...] == c + lax.broadcasted_iota(jnp.int32, (rows, chunk), 1)
            sign = jnp.where(match, -1.0, 1.0)
            tile = sign * pltpu.reciprocal(
                floor + floor * jnp.exp2(sign * power), approx=True
            )
        else:
            tile = pltpu.reciprocal(floor + floor * jnp.exp2(power), approx=True)
        grads.append(tile.astype(jnp.bfloat16))
    grad = grads[0] if len(grads) == 1 else jnp.concatenate(grads, 1)
    total = jnp.dot(grad, unit_ref[...], preferred_element_type=jnp.float32)
    if has_sum:
        total = total + sum_ref[...]
    if final:
        norm = norm_ref[...]
        unit = raw_ref[...].astype(jnp.float32) * norm
        total = norm * (total - unit * jnp.sum(unit * total, -1, keepdims=True))
    out_ref[...] = total


def one_side(
    scalars, own, other, pair=None, label=None, raw_other=False, so_far=None, final=None, step=512,
    chunk=256, name="side",
):
    rows, width = own.shape
    count = other.shape[0]
    block = pl.BlockSpec((step, width), lambda i: (i, 0))
    column = pl.BlockSpec((step, 1), lambda i: (i, 0))
    whole = pl.BlockSpec((count, width), lambda i: (0, 0))
    args = [scalars, own, other]
    specs = [pl.BlockSpec(memory_space=pltpu.SMEM), block, whole]
    if label:
        args.append(pair)
        specs.append(column if label == "column" else pl.BlockSpec((1, count), lambda i: (0, 0)))
    if so_far is not None:
        args.append(so_far)
        specs.append(block)
    if final is not None:
        args += list(final)
        specs += [block, column]
    kernel = functools.partial(
        side_kernel, label=label, raw_other=raw_other, has_sum=so_far is not None,
        final=final is not None, chunk=chunk,
    )
    return pl.pallas_call(
        kernel,
        grid=(rows // step,),
        in_specs=specs,
        out_specs=block,
        out_shape=jax.ShapeDtypeStruct((rows, width), jnp.float32),
        scratch_shapes=[pltpu.VMEM((count, width), jnp.bfloat16)] if raw_other else [],
        compiler_params=pltpu.CompilerParams(vmem_limit_bytes=VMEM_LIMIT),
        cost_estimate=pl.CostEstimate(
            flops=rows * width, bytes_accessed=rows * width, transcendentals=0
        ),
        name=name,
    )(*args)


def local(
    photo_vectors_raw, sentence_vectors_raw, companion_index, exponent_of_sharpness, affinity_offset
):
    sharpness = jnp.exp(exponent_of_sharpness[0])
    scalars = jnp.stack([-LOG2E * sharpness, -LOG2E * affinity_offset[0], 1.0 / sharpness])
    rows = photo_vectors_raw.shape[0]

    text_near = swapped(sentence_vectors_raw, 0)
    text_far = swapped(sentence_vectors_raw, 1)
    image_unit, image_norm, text_unit, text_norm = prepare(photo_vectors_raw, sentence_vectors_raw)
    image_near = swapped(image_unit, 0)
    image_far = swapped(image_unit, 1)

    image_sum = one_side(
        scalars, image_unit, text_unit, companion_index.reshape(rows, 1), "column", name="image_own"
    )
    text_sum = one_side(scalars, text_unit, image_unit, companion_index, "row", name="text_own")
    image_sum = one_side(
        scalars, image_unit, text_near, raw_other=True, so_far=image_sum, name="image_near"
    )
    image_grad = one_side(
        scalars, image_unit, text_far, raw_other=True, so_far=image_sum,
        final=(photo_vectors_raw, image_norm), name="image_far",
    )
    image_grad, text_sum = lax.optimization_barrier((image_grad, text_sum))
    text_sum = one_side(scalars, text_unit, image_near, so_far=text_sum, name="text_near")
    text_grad = one_side(
        scalars, text_unit, image_far, so_far=text_sum, final=(sentence_vectors_raw, text_norm),
        name="text_far",
    )
    return (image_grad, text_grad)


def solution(mesh):
    placed = (P(AXES, None), P(AXES, None), P(AXES, None), P(), P())
    return jax.shard_map(
        local, mesh=mesh, in_specs=placed, out_specs=(P(AXES, None), P(AXES, None)), check_vma=False
    )
```

```python
import functools

import jax
import jax.numpy as jnp
from jax import lax
from jax.experimental import pallas as pl
from jax.experimental.pallas import tpu as pltpu
from jax.sharding import PartitionSpec as P

AXES = ("grp", "dp")
LOG2E = 1.4426950408889634
VMEM_LIMIT = 24 * 2**20
LAST = 4
IN_VMEM = pl.BlockSpec(memory_space=pltpu.VMEM)
IN_SMEM = pl.BlockSpec(memory_space=pltpu.SMEM)


def swapped(x, parity):
    devices = lax.axis_size(AXES)
    pairs = []
    for k in range(parity, devices, 2):
        after = (k + 1) % devices
        pairs += [(k, after), (after, k)]
    return lax.ppermute(x, AXES, pairs)


def unit_rows(raw):
    values = raw.astype(jnp.float32)
    norm = lax.rsqrt(jnp.sum(values * values, -1, keepdims=True) + 1e-06)
    return values * norm, norm


def prepare_kernel(image, text, image_out, head_out, tail_out, image_norm, text_out, text_norm):
    rows, step = image.shape[0], 256
    head = head_out.shape[0]
    for r in range(0, rows, step):
        at = slice(r, r + step)
        unit, image_norm[at, :] = unit_rows(image[at, :])
        unit = unit.astype(jnp.bfloat16)
        image_out[at, :] = unit
        if r < head:
            head_out[at, :] = unit
        else:
            tail_out[r - head : r - head + step, :] = unit
        unit, text_norm[at, :] = unit_rows(text[at, :])
        text_out[at, :] = unit.astype(jnp.bfloat16)


def prepare(image, text):
    rows, width = image.shape
    last = rows // LAST
    unit = jax.ShapeDtypeStruct((rows, width), jnp.bfloat16)
    head = jax.ShapeDtypeStruct((rows - last, width), jnp.bfloat16)
    tail = jax.ShapeDtypeStruct((last, width), jnp.bfloat16)
    norm = jax.ShapeDtypeStruct((rows, 1), jnp.float32)
    return pl.pallas_call(
        prepare_kernel,
        in_specs=[IN_VMEM, IN_VMEM],
        out_specs=[IN_VMEM] * 6,
        out_shape=[unit, head, tail, norm, unit, norm],
        compiler_params=pltpu.CompilerParams(vmem_limit_bytes=VMEM_LIMIT),
        cost_estimate=pl.CostEstimate(
            flops=8 * rows * width, bytes_accessed=8 * rows * width, transcendentals=2 * rows
        ),
        name="prepare",
    )(image, text)


def side_kernel(*refs, label, raw_other, has_sum, final, step, chunk):
    refs = list(refs)
    scalars, own_ref, other_ref = refs[:3]
    refs = refs[3:]
    pair_ref = refs.pop(0) if label else None
    sum_ref = refs.pop(0) if has_sum else None
    raw_ref, norm_ref = (refs.pop(0), refs.pop(0)) if final else (None, None)
    out_ref = refs.pop(0)
    rows, count = own_ref.shape[0], other_ref.shape[0]
    if raw_other:
        unit_ref = refs.pop(0)
        for r in range(0, count, 256):
            unit, _ = unit_rows(other_ref[r : r + 256, :])
            unit_ref[r : r + 256, :] = unit.astype(jnp.bfloat16)
    else:
        unit_ref = other_ref
    if final:
        grad_ref, sem = refs
    slope, shift, floor = scalars[0], scalars[1], scalars[2]
    for r in range(0, rows, step):
        at = slice(r, r + step)
        own = own_ref[at, :]
        tiles = []
        for c in range(0, count, chunk):
            scores = lax.dot_general(
                own,
                unit_ref[c : c + chunk, :],
                (((1,), (1,)), ((), ())),
                preferred_element_type=jnp.float32,
            )
            power = slope * scores + shift
            if label:
                if label == "row":
                    row_id = r + lax.broadcasted_iota(jnp.int32, (step, chunk), 0)
                    match = row_id == pair_ref[:, c : c + chunk]
                else:
                    column_id = c + lax.broadcasted_iota(jnp.int32, (step, chunk), 1)
                    match = pair_ref[at, :] == column_id
                sign = jnp.where(match, -1.0, 1.0)
                tile = sign * pltpu.reciprocal(
                    floor + floor * jnp.exp2(sign * power), approx=True
                )
            else:
                tile = pltpu.reciprocal(floor + floor * jnp.exp2(power), approx=True)
            tiles.append(tile.astype(jnp.bfloat16))
        tile = tiles[0] if len(tiles) == 1 else jnp.concatenate(tiles, 1)
        total = jnp.dot(tile, unit_ref[...], preferred_element_type=jnp.float32)
        if has_sum:
            total = total + sum_ref[at, :]
        if final:
            norm = norm_ref[at, :]
            unit = raw_ref[at, :].astype(jnp.float32) * norm
            total = norm * (total - unit * jnp.sum(unit * total, -1, keepdims=True))
            grad_ref[at, :] = total
            pltpu.make_async_copy(grad_ref.at[at], out_ref.at[at], sem.at[r // step]).start()
        else:
            out_ref[at, :] = total
    if final:
        for r in range(0, rows, step):
            at = slice(r, r + step)
            pltpu.make_async_copy(grad_ref.at[at], out_ref.at[at], sem.at[r // step]).wait()


def one_side(
    scalars, own, other, pair=None, label=None, raw_other=False, so_far=None, final=None, step=256,
    chunk=256, name="side",
):
    rows, width = own.shape
    count = other.shape[0]
    args = [scalars, own, other]
    if label:
        args.append(pair)
    if so_far is not None:
        args.append(so_far)
    scratch = []
    if raw_other:
        scratch.append(pltpu.VMEM((count, width), jnp.bfloat16))
    if final is not None:
        args += list(final)
        scratch.append(pltpu.VMEM((rows, width), jnp.float32))
        scratch.append(pltpu.SemaphoreType.DMA((rows // step,)))
    kernel = functools.partial(
        side_kernel, label=label, raw_other=raw_other, has_sum=so_far is not None,
        final=final is not None, step=step, chunk=min(chunk, count),
    )
    return pl.pallas_call(
        kernel,
        in_specs=[IN_SMEM] + [IN_VMEM] * (len(args) - 1),
        out_specs=IN_VMEM if final is None else pl.BlockSpec(memory_space=pl.ANY),
        out_shape=jax.ShapeDtypeStruct((rows, width), jnp.float32),
        scratch_shapes=scratch,
        compiler_params=pltpu.CompilerParams(vmem_limit_bytes=VMEM_LIMIT),
        cost_estimate=pl.CostEstimate(
            flops=rows * width, bytes_accessed=rows * width, transcendentals=0
        ),
        name=name,
    )(*args)


def local(
    photo_vectors_raw, sentence_vectors_raw, companion_index, exponent_of_sharpness, affinity_offset
):
    sharpness = jnp.exp(exponent_of_sharpness[0])
    scalars = jnp.stack([-LOG2E * sharpness, -LOG2E * affinity_offset[0], 1.0 / sharpness])
    rows = photo_vectors_raw.shape[0]

    text_far = swapped(sentence_vectors_raw, 1)
    text_near = swapped(sentence_vectors_raw, 0)
    image_unit, image_head, image_tail, image_norm, text_unit, text_norm = prepare(
        photo_vectors_raw, sentence_vectors_raw
    )
    image_near = swapped(image_unit, 0)
    head_far = swapped(image_head, 1)
    tail_far = swapped(image_tail, 1)

    image_sum = one_side(
        scalars, image_unit, text_unit, companion_index.reshape(rows, 1), "column", name="image_own"
    )
    text_sum = one_side(scalars, text_unit, image_unit, companion_index, "row", name="text_own")
    image_sum = one_side(
        scalars, image_unit, text_near, raw_other=True, so_far=image_sum, name="image_near"
    )
    image_grad = one_side(
        scalars, image_unit, text_far, raw_other=True, so_far=image_sum,
        final=(photo_vectors_raw, image_norm), name="image_far",
    )
    image_grad, text_sum = lax.optimization_barrier((image_grad, text_sum))
    text_sum = one_side(scalars, text_unit, image_near, so_far=text_sum, name="text_near")
    text_sum = one_side(scalars, text_unit, head_far, so_far=text_sum, name="text_far_head")
    text_grad = one_side(
        scalars, text_unit, tail_far, so_far=text_sum, final=(sentence_vectors_raw, text_norm),
        name="text_far_tail",
    )
    return (image_grad, text_grad)


def solution(mesh):
    placed = (P(AXES, None), P(AXES, None), P(AXES, None), P(), P())
    return jax.shard_map(
        local, mesh=mesh, in_specs=placed, out_specs=(P(AXES, None), P(AXES, None)), check_vma=False
    )
```

```python
import functools

import jax
import jax.numpy as jnp
from jax import lax
from jax.experimental import pallas as pl
from jax.experimental.pallas import tpu as pltpu
from jax.sharding import PartitionSpec as P

AXES = ("grp", "dp")
LOG2E = 1.4426950408889634
VMEM_LIMIT = 24 * 2**20
NEAR_LAST, FAR_LAST = 2, 4
IN_VMEM = pl.BlockSpec(memory_space=pltpu.VMEM)
IN_SMEM = pl.BlockSpec(memory_space=pltpu.SMEM)


def swapped(x, parity):
    devices = lax.axis_size(AXES)
    pairs = []
    for k in range(parity, devices, 2):
        after = (k + 1) % devices
        pairs += [(k, after), (after, k)]
    return lax.ppermute(x, AXES, pairs)


def unit_rows(raw):
    values = raw.astype(jnp.float32)
    norm = lax.rsqrt(jnp.sum(values * values, -1, keepdims=True) + 1e-06)
    return values * norm, norm


def prepare_kernel(image, text, *outs):
    image_out, image_norm, text_out, text_norm, *parts = outs
    rows, step = image.shape[0], 256
    for r in range(0, rows, step):
        at = slice(r, r + step)
        unit, image_norm[at, :] = unit_rows(image[at, :])
        unit = unit.astype(jnp.bfloat16)
        image_out[at, :] = unit
        for head, tail in (parts[:2], parts[2:]):
            count = head.shape[0]
            if r < count:
                head[at, :] = unit
            else:
                tail[r - count : r - count + step, :] = unit
        unit, text_norm[at, :] = unit_rows(text[at, :])
        text_out[at, :] = unit.astype(jnp.bfloat16)


def prepare(image, text):
    rows, width = image.shape
    unit = jax.ShapeDtypeStruct((rows, width), jnp.bfloat16)
    norm = jax.ShapeDtypeStruct((rows, 1), jnp.float32)
    parts = []
    for last in (rows // NEAR_LAST, rows // FAR_LAST):
        parts.append(jax.ShapeDtypeStruct((rows - last, width), jnp.bfloat16))
        parts.append(jax.ShapeDtypeStruct((last, width), jnp.bfloat16))
    return pl.pallas_call(
        prepare_kernel,
        in_specs=[IN_VMEM, IN_VMEM],
        out_specs=[IN_VMEM] * 8,
        out_shape=[unit, norm, unit, norm] + parts,
        compiler_params=pltpu.CompilerParams(vmem_limit_bytes=VMEM_LIMIT),
        cost_estimate=pl.CostEstimate(
            flops=8 * rows * width, bytes_accessed=8 * rows * width, transcendentals=2 * rows
        ),
        name="prepare",
    )(image, text)


def side_kernel(*refs, label, raw_other, has_sum, final, step, chunk):
    refs = list(refs)
    scalars, own_ref, other_ref = refs[:3]
    refs = refs[3:]
    pair_ref = refs.pop(0) if label else None
    sum_ref = refs.pop(0) if has_sum else None
    raw_ref, norm_ref = (refs.pop(0), refs.pop(0)) if final else (None, None)
    out_ref = refs.pop(0)
    rows, count = own_ref.shape[0], other_ref.shape[0]
    if raw_other:
        unit_ref = refs.pop(0)
        for r in range(0, count, 256):
            unit, _ = unit_rows(other_ref[r : r + 256, :])
            unit_ref[r : r + 256, :] = unit.astype(jnp.bfloat16)
    else:
        unit_ref = other_ref
    if final:
        grad_ref, sem = refs
    slope, shift, floor, log_floor = (scalars[i] for i in range(4))

    def scores(r):
        own = own_ref[r : r + step, :]
        return [
            lax.dot_general(
                own,
                unit_ref[c : c + chunk, :],
                (((1,), (1,)), ((), ())),
                preferred_element_type=jnp.float32,
            )
            for c in range(0, count, chunk)
        ]

    def grad_tile(r, c, scores):
        power = slope * scores + shift
        if not label:
            tile = pltpu.reciprocal(floor + jnp.exp2(power + log_floor), approx=True)
        else:
            if label == "row":
                row_id = r + lax.broadcasted_iota(jnp.int32, (step, chunk), 0)
                match = row_id == pair_ref[:, c : c + chunk]
            else:
                column_id = c + lax.broadcasted_iota(jnp.int32, (step, chunk), 1)
                match = pair_ref[r : r + step, :] == column_id
            sign = jnp.where(match, -1.0, 1.0)
            tile = sign * pltpu.reciprocal(
                floor + jnp.exp2(sign * power + log_floor), approx=True
            )
        return tile.astype(jnp.bfloat16)

    coming = scores(0)
    for r in range(0, rows, step):
        at = slice(r, r + step)
        now, coming = coming, scores(r + step) if r + step < rows else None
        tiles = [grad_tile(r, i * chunk, part) for i, part in enumerate(now)]
        tile = tiles[0] if len(tiles) == 1 else jnp.concatenate(tiles, 1)
        total = jnp.dot(tile, unit_ref[...], preferred_element_type=jnp.float32)
        if has_sum:
            total = total + sum_ref[at, :]
        if final:
            norm = norm_ref[at, :]
            unit = raw_ref[at, :].astype(jnp.float32) * norm
            total = norm * (total - unit * jnp.sum(unit * total, -1, keepdims=True))
            grad_ref[at, :] = total
            pltpu.make_async_copy(grad_ref.at[at], out_ref.at[at], sem.at[r // step]).start()
        else:
            out_ref[at, :] = total
    if final:
        for r in range(0, rows, step):
            at = slice(r, r + step)
            pltpu.make_async_copy(grad_ref.at[at], out_ref.at[at], sem.at[r // step]).wait()


def one_side(
    scalars, own, other, pair=None, label=None, raw_other=False, so_far=None, final=None, step=256,
    chunk=256, name="side",
):
    rows, width = own.shape
    count = other.shape[0]
    args = [scalars, own, other]
    if label:
        args.append(pair)
    if so_far is not None:
        args.append(so_far)
    scratch = []
    if raw_other:
        scratch.append(pltpu.VMEM((count, width), jnp.bfloat16))
    if final is not None:
        args += list(final)
        scratch.append(pltpu.VMEM((rows, width), jnp.float32))
        scratch.append(pltpu.SemaphoreType.DMA((rows // step,)))
    kernel = functools.partial(
        side_kernel, label=label, raw_other=raw_other, has_sum=so_far is not None,
        final=final is not None, step=step, chunk=min(chunk, count),
    )
    return pl.pallas_call(
        kernel,
        in_specs=[IN_SMEM] + [IN_VMEM] * (len(args) - 1),
        out_specs=IN_VMEM if final is None else pl.BlockSpec(memory_space=pl.ANY),
        out_shape=jax.ShapeDtypeStruct((rows, width), jnp.float32),
        scratch_shapes=scratch,
        compiler_params=pltpu.CompilerParams(vmem_limit_bytes=VMEM_LIMIT),
        cost_estimate=pl.CostEstimate(
            flops=rows * width, bytes_accessed=rows * width, transcendentals=0
        ),
        name=name,
    )(*args)


def local(
    photo_vectors_raw, sentence_vectors_raw, companion_index, exponent_of_sharpness, affinity_offset
):
    exponent, offset = exponent_of_sharpness[0], affinity_offset[0]
    scalars = jnp.stack(
        [-LOG2E * jnp.exp(exponent), -LOG2E * offset, jnp.exp(-exponent), -LOG2E * exponent]
    )
    rows = photo_vectors_raw.shape[0]

    text_far = swapped(sentence_vectors_raw, 1)
    text_near = swapped(sentence_vectors_raw, 0)
    image_unit, image_norm, text_unit, text_norm, *parts = prepare(
        photo_vectors_raw, sentence_vectors_raw
    )
    near_head, near_tail = (swapped(part, 0) for part in parts[:2])
    far_head = swapped(parts[2], 1)

    text_sum = one_side(scalars, text_unit, image_unit, companion_index, "row", name="text_own")
    image_sum = one_side(
        scalars, image_unit, text_unit, companion_index.reshape(rows, 1), "column", name="image_own"
    )
    image_sum, text_sum, far_part = lax.optimization_barrier((image_sum, text_sum, parts[3]))
    far_tail = swapped(far_part, 1)
    image_sum = one_side(
        scalars, image_unit, text_near, raw_other=True, so_far=image_sum, name="image_near"
    )
    image_sum, text_sum = lax.optimization_barrier((image_sum, text_sum))
    text_sum = one_side(scalars, text_unit, near_head, so_far=text_sum, name="text_near_head")
    image_sum, text_sum = lax.optimization_barrier((image_sum, text_sum))
    image_grad = one_side(
        scalars, image_unit, text_far, raw_other=True, so_far=image_sum,
        final=(photo_vectors_raw, image_norm), name="image_far",
    )
    image_grad, text_sum = lax.optimization_barrier((image_grad, text_sum))
    text_sum = one_side(scalars, text_unit, near_tail, so_far=text_sum, name="text_near_tail")
    text_sum = one_side(scalars, text_unit, far_head, so_far=text_sum, name="text_far_head")
    text_grad = one_side(
        scalars, text_unit, far_tail, so_far=text_sum, final=(sentence_vectors_raw, text_norm),
        name="text_far_tail",
    )
    return (image_grad, text_grad)


def solution(mesh):
    placed = (P(AXES, None), P(AXES, None), P(AXES, None), P(), P())
    return jax.shard_map(
        local, mesh=mesh, in_specs=placed, out_specs=(P(AXES, None), P(AXES, None)), check_vma=False
    )
```

```python
import functools

import jax
import jax.numpy as jnp
from jax import lax
from jax.experimental import pallas as pl
from jax.experimental.pallas import tpu as pltpu
from jax.sharding import PartitionSpec as P

AXES = ("grp", "dp")
LOG2E = 1.4426950408889634
VMEM_LIMIT = 24 * 2**20
NEAR_LAST, FAR_LAST = 2, 4
IN_VMEM = pl.BlockSpec(memory_space=pltpu.VMEM)
ANYWHERE = pl.BlockSpec(memory_space=pl.ANY)
IN_SMEM = pl.BlockSpec(memory_space=pltpu.SMEM)


def swapped(x, parity):
    devices = lax.axis_size(AXES)
    pairs = []
    for k in range(parity, devices, 2):
        after = (k + 1) % devices
        pairs += [(k, after), (after, k)]
    return lax.ppermute(x, AXES, pairs)


def unit_rows(raw):
    values = raw.astype(jnp.float32)
    norm = lax.rsqrt(jnp.sum(values * values, -1, keepdims=True) + 1e-06)
    return values * norm, norm


def prepare_kernel(image, text, *outs):
    image_out, image_norm, text_out, text_norm, *parts = outs
    rows, step = image.shape[0], 256
    for r in range(0, rows, step):
        at = slice(r, r + step)
        unit, image_norm[at, :] = unit_rows(image[at, :])
        unit = unit.astype(jnp.bfloat16)
        image_out[at, :] = unit
        for head, tail in (parts[:2], parts[2:]):
            count = head.shape[0]
            if r < count:
                head[at, :] = unit
            else:
                tail[r - count : r - count + step, :] = unit
        unit, text_norm[at, :] = unit_rows(text[at, :])
        text_out[at, :] = unit.astype(jnp.bfloat16)


def prepare(image, text):
    rows, width = image.shape
    unit = jax.ShapeDtypeStruct((rows, width), jnp.bfloat16)
    norm = jax.ShapeDtypeStruct((rows, 1), jnp.float32)
    parts = []
    for last in (rows // NEAR_LAST, rows // FAR_LAST):
        parts.append(jax.ShapeDtypeStruct((rows - last, width), jnp.bfloat16))
        parts.append(jax.ShapeDtypeStruct((last, width), jnp.bfloat16))
    return pl.pallas_call(
        prepare_kernel,
        in_specs=[IN_VMEM, IN_VMEM],
        out_specs=[IN_VMEM] * 8,
        out_shape=[unit, norm, unit, norm] + parts,
        compiler_params=pltpu.CompilerParams(vmem_limit_bytes=VMEM_LIMIT),
        cost_estimate=pl.CostEstimate(
            flops=8 * rows * width, bytes_accessed=8 * rows * width, transcendentals=2 * rows
        ),
        name="prepare",
    )(image, text)


def side_kernel(*refs, label, raw_other, has_sum, final, late, step, chunk):
    refs = list(refs)
    scalars, own_ref, other_ref = refs[:3]
    refs = refs[3:]
    pair_ref = refs.pop(0) if label else None
    sum_ref = refs.pop(0) if has_sum else None
    raw_ref, norm_ref = (refs.pop(0), refs.pop(0)) if final else (None, None)
    out_ref = refs.pop(0)
    rows, count = own_ref.shape[0], other_ref.shape[0]
    if raw_other:
        unit_ref = refs.pop(0)
        for r in range(0, count, 256):
            unit, _ = unit_rows(other_ref[r : r + 256, :])
            unit_ref[r : r + 256, :] = unit.astype(jnp.bfloat16)
    else:
        unit_ref = other_ref
    if final:
        grad_ref, sem = refs[:2]
    if late:
        late_ref, late_sem = refs[2:]
        fetch = pltpu.make_async_copy(raw_ref, late_ref, late_sem)
        fetch.start()
        raw_ref = late_ref
    slope, shift, floor, log_floor = (scalars[i] for i in range(4))

    def scores(r):
        own = own_ref[r : r + step, :]
        return [
            lax.dot_general(
                own,
                unit_ref[c : c + chunk, :],
                (((1,), (1,)), ((), ())),
                preferred_element_type=jnp.float32,
            )
            for c in range(0, count, chunk)
        ]

    def grad_tile(r, c, scores):
        power = slope * scores + shift
        if not label:
            tile = pltpu.reciprocal(floor + jnp.exp2(power + log_floor), approx=True)
        else:
            if label == "row":
                row_id = r + lax.broadcasted_iota(jnp.int32, (step, chunk), 0)
                match = row_id == pair_ref[:, c : c + chunk]
            else:
                column_id = c + lax.broadcasted_iota(jnp.int32, (step, chunk), 1)
                match = pair_ref[r : r + step, :] == column_id
            sign = jnp.where(match, -1.0, 1.0)
            tile = sign * pltpu.reciprocal(
                floor + jnp.exp2(sign * power + log_floor), approx=True
            )
        return tile.astype(jnp.bfloat16)

    coming = scores(0)
    for r in range(0, rows, step):
        at = slice(r, r + step)
        now, coming = coming, scores(r + step) if r + step < rows else None
        tiles = [grad_tile(r, i * chunk, part) for i, part in enumerate(now)]
        tile = tiles[0] if len(tiles) == 1 else jnp.concatenate(tiles, 1)
        total = jnp.dot(tile, unit_ref[...], preferred_element_type=jnp.float32)
        if has_sum:
            total = total + sum_ref[at, :]
        if late and r == 0:
            fetch.wait()
        if final:
            norm = norm_ref[at, :]
            unit = raw_ref[at, :].astype(jnp.float32) * norm
            total = norm * (total - unit * jnp.sum(unit * total, -1, keepdims=True))
            grad_ref[at, :] = total
            pltpu.make_async_copy(grad_ref.at[at], out_ref.at[at], sem.at[r // step]).start()
        else:
            out_ref[at, :] = total
    if final:
        for r in range(0, rows, step):
            at = slice(r, r + step)
            pltpu.make_async_copy(grad_ref.at[at], out_ref.at[at], sem.at[r // step]).wait()


def one_side(
    scalars, own, other, pair=None, label=None, raw_other=False, so_far=None, final=None, late=False,
    step=256, chunk=256, name="side",
):
    rows, width = own.shape
    count = other.shape[0]
    args = [scalars, own, other]
    if label:
        args.append(pair)
    if so_far is not None:
        args.append(so_far)
    scratch = []
    if raw_other:
        scratch.append(pltpu.VMEM((count, width), jnp.bfloat16))
    specs = [IN_SMEM] + [IN_VMEM] * (len(args) - 1)
    if final is not None:
        args += list(final)
        specs += [ANYWHERE if late else IN_VMEM, IN_VMEM]
        scratch.append(pltpu.VMEM((rows, width), jnp.float32))
        scratch.append(pltpu.SemaphoreType.DMA((rows // step,)))
    if late:
        scratch += [pltpu.VMEM((rows, width), jnp.bfloat16), pltpu.SemaphoreType.DMA]
    kernel = functools.partial(
        side_kernel, label=label, raw_other=raw_other, has_sum=so_far is not None,
        final=final is not None, late=late, step=step, chunk=min(chunk, count),
    )
    return pl.pallas_call(
        kernel,
        in_specs=specs,
        out_specs=IN_VMEM if final is None else ANYWHERE,
        out_shape=jax.ShapeDtypeStruct((rows, width), jnp.float32),
        scratch_shapes=scratch,
        input_output_aliases={len(args) - 1: 0} if so_far is not None and final is None else {},
        compiler_params=pltpu.CompilerParams(vmem_limit_bytes=VMEM_LIMIT),
        cost_estimate=pl.CostEstimate(
            flops=rows * width, bytes_accessed=rows * width, transcendentals=0
        ),
        name=name,
    )(*args)


def local(
    photo_vectors_raw, sentence_vectors_raw, companion_index, exponent_of_sharpness, affinity_offset
):
    exponent, offset = exponent_of_sharpness[0], affinity_offset[0]
    scalars = jnp.stack(
        [-LOG2E * jnp.exp(exponent), -LOG2E * offset, jnp.exp(-exponent), -LOG2E * exponent]
    )
    rows = photo_vectors_raw.shape[0]

    text_far = swapped(sentence_vectors_raw, 1)
    text_near = swapped(sentence_vectors_raw, 0)
    image_unit, image_norm, text_unit, text_norm, *parts = prepare(
        photo_vectors_raw, sentence_vectors_raw
    )
    text_sum = one_side(scalars, text_unit, image_unit, companion_index, "row", name="text_own")
    text_sum, near_part, image_unit = lax.optimization_barrier((text_sum, parts[0], image_unit))
    near_head = swapped(near_part, 0)
    image_sum = one_side(
        scalars, image_unit, text_unit, companion_index.reshape(rows, 1), "column", name="image_own"
    )
    image_sum, far_part = lax.optimization_barrier((image_sum, parts[2]))
    far_head = swapped(far_part, 1)
    image_sum = one_side(
        scalars, image_unit, text_near, raw_other=True, so_far=image_sum, name="image_near"
    )
    image_sum, text_sum, near_part, far_part = lax.optimization_barrier(
        (image_sum, text_sum, parts[1], parts[3])
    )
    near_tail = swapped(near_part, 0)
    far_tail = swapped(far_part, 1)
    text_sum = one_side(scalars, text_unit, near_head, so_far=text_sum, name="text_near_head")
    image_sum, text_sum = lax.optimization_barrier((image_sum, text_sum))
    image_grad = one_side(
        scalars, image_unit, text_far, raw_other=True, so_far=image_sum,
        final=(photo_vectors_raw, image_norm), late=True, name="image_far",
    )
    image_grad, text_sum = lax.optimization_barrier((image_grad, text_sum))
    text_sum = one_side(scalars, text_unit, near_tail, so_far=text_sum, name="text_near_tail")
    text_sum = one_side(scalars, text_unit, far_head, so_far=text_sum, name="text_far_head")
    text_grad = one_side(
        scalars, text_unit, far_tail, so_far=text_sum, final=(sentence_vectors_raw, text_norm),
        name="text_far_tail",
    )
    return (image_grad, text_grad)


def solution(mesh):
    placed = (P(AXES, None), P(AXES, None), P(AXES, None), P(), P())
    return jax.shard_map(
        local, mesh=mesh, in_specs=placed, out_specs=(P(AXES, None), P(AXES, None)), check_vma=False
    )
```

```python
import functools

import jax
import jax.numpy as jnp
from jax import lax
from jax.experimental import pallas as pl
from jax.experimental.pallas import tpu as pltpu
from jax.sharding import PartitionSpec as P

AXES = ("grp", "dp")
LOG2E = 1.4426950408889634
VMEM_LIMIT = 24 * 2**20
NEAR_LAST, FAR_LAST = 512, 256
IN_VMEM = pl.BlockSpec(memory_space=pltpu.VMEM)
ANYWHERE = pl.BlockSpec(memory_space=pl.ANY)
IN_SMEM = pl.BlockSpec(memory_space=pltpu.SMEM)


def swapped(x, parity):
    devices = lax.axis_size(AXES)
    pairs = []
    for k in range(parity, devices, 2):
        after = (k + 1) % devices
        pairs += [(k, after), (after, k)]
    return lax.ppermute(x, AXES, pairs)


def unit_rows(raw):
    values = raw.astype(jnp.float32)
    norm = lax.rsqrt(jnp.sum(values * values, -1, keepdims=True) + 1e-06)
    return values * norm, norm


def prepare_kernel(image, text, *outs):
    image_out, image_norm, text_out, text_norm, *parts = outs
    rows, step = image.shape[0], 128
    for r in range(0, rows, step):
        at = slice(r, r + step)
        unit, image_norm[at, :] = unit_rows(image[at, :])
        unit = unit.astype(jnp.bfloat16)
        image_out[at, :] = unit
        for head, tail in (parts[:2], parts[2:]):
            count = head.shape[0]
            if r < count:
                head[at, :] = unit
            else:
                tail[r - count : r - count + step, :] = unit
        unit, text_norm[at, :] = unit_rows(text[at, :])
        text_out[at, :] = unit.astype(jnp.bfloat16)


def prepare(image, text):
    rows, width = image.shape
    unit = jax.ShapeDtypeStruct((rows, width), jnp.bfloat16)
    norm = jax.ShapeDtypeStruct((rows, 1), jnp.float32)
    parts = []
    for last in (NEAR_LAST, FAR_LAST):
        parts.append(jax.ShapeDtypeStruct((rows - last, width), jnp.bfloat16))
        parts.append(jax.ShapeDtypeStruct((last, width), jnp.bfloat16))
    return pl.pallas_call(
        prepare_kernel,
        in_specs=[IN_VMEM, IN_VMEM],
        out_specs=[IN_VMEM] * 8,
        out_shape=[unit, norm, unit, norm] + parts,
        compiler_params=pltpu.CompilerParams(vmem_limit_bytes=VMEM_LIMIT),
        cost_estimate=pl.CostEstimate(
            flops=8 * rows * width, bytes_accessed=8 * rows * width, transcendentals=2 * rows
        ),
        name="prepare",
    )(image, text)


def side_kernel(*refs, label, raw_other, has_sum, finish, written, late, step, chunk):
    refs = list(refs)
    scalars, own_ref, other_ref = refs[:3]
    refs = refs[3:]
    pair_ref = refs.pop(0) if label else None
    sum_ref = refs.pop(0) if has_sum else None
    raw_ref, norm_ref = (refs.pop(0), refs.pop(0)) if finish else (None, None)
    out_ref = refs.pop(0)
    rows, count = own_ref.shape[0], other_ref.shape[0]
    if raw_other:
        unit_ref = refs.pop(0)
        for r in range(0, count, 256):
            unit, _ = unit_rows(other_ref[r : r + 256, :])
            unit_ref[r : r + 256, :] = unit.astype(jnp.bfloat16)
    else:
        unit_ref = other_ref
    if written:
        grad_ref, sem = refs[:2]
    if late:
        late_ref, late_sem = refs[2:]
        fetch = pltpu.make_async_copy(raw_ref, late_ref, late_sem)
        fetch.start()
        raw_ref = late_ref
    slope, shift, floor, log_floor = (scalars[i] for i in range(4))

    def scores(r):
        own = own_ref[r : r + step, :]
        return [
            lax.dot_general(
                own,
                unit_ref[c : c + chunk, :],
                (((1,), (1,)), ((), ())),
                preferred_element_type=jnp.float32,
            )
            for c in range(0, count, chunk)
        ]

    def grad_tile(r, c, scores):
        power = slope * scores + shift
        if not label:
            tile = pltpu.reciprocal(floor + jnp.exp2(power + log_floor), approx=True)
        else:
            if label == "row":
                row_id = r + lax.broadcasted_iota(jnp.int32, (step, chunk), 0)
                match = row_id == pair_ref[:, c : c + chunk]
            else:
                column_id = c + lax.broadcasted_iota(jnp.int32, (step, chunk), 1)
                match = pair_ref[r : r + step, :] == column_id
            sign = jnp.where(match, -1.0, 1.0)
            tile = sign * pltpu.reciprocal(
                floor + jnp.exp2(sign * power + log_floor), approx=True
            )
        return tile.astype(jnp.bfloat16)

    coming = scores(0)
    for r in range(0, rows, step):
        at = slice(r, r + step)
        now, coming = coming, scores(r + step) if r + step < rows else None
        tiles = [grad_tile(r, i * chunk, part) for i, part in enumerate(now)]
        tile = tiles[0] if len(tiles) == 1 else jnp.concatenate(tiles, 1)
        total = jnp.dot(tile, unit_ref[...], preferred_element_type=jnp.float32)
        if late and r == 0:
            fetch.wait()
        if finish == "more":
            along = sum(
                jnp.sum(piece.astype(jnp.float32) * part, -1, keepdims=True)
                for piece, part in zip(tiles, now)
            )
            norm = norm_ref[at, :]
            raw = raw_ref[at, :].astype(jnp.float32)
            total = sum_ref[at, :] + norm * total - (norm * norm * along) * raw
        elif has_sum:
            total = total + sum_ref[at, :]
        if finish == "whole":
            norm = norm_ref[at, :]
            unit = raw_ref[at, :].astype(jnp.float32) * norm
            total = norm * (total - unit * jnp.sum(unit * total, -1, keepdims=True))
        if written:
            grad_ref[at, :] = total
            pltpu.make_async_copy(grad_ref.at[at], out_ref.at[at], sem.at[r // step]).start()
        else:
            out_ref[at, :] = total
    if written:
        for r in range(0, rows, step):
            at = slice(r, r + step)
            pltpu.make_async_copy(grad_ref.at[at], out_ref.at[at], sem.at[r // step]).wait()


def one_side(
    scalars, own, other, pair=None, label=None, raw_other=False, so_far=None, finish=None, rows_of=(),
    written=False, late=False, step=256, chunk=256, name="side",
):
    rows, width = own.shape
    count = other.shape[0]
    args = [scalars, own, other]
    if label:
        args.append(pair)
    if so_far is not None:
        args.append(so_far)
    sum_at = len(args) - 1
    specs = [IN_SMEM] + [IN_VMEM] * sum_at
    if finish:
        args += list(rows_of)
        specs += [ANYWHERE if late else IN_VMEM, IN_VMEM]
    scratch = []
    if raw_other:
        scratch.append(pltpu.VMEM((count, width), jnp.bfloat16))
    if written:
        scratch.append(pltpu.VMEM((rows, width), jnp.float32))
        scratch.append(pltpu.SemaphoreType.DMA((rows // step,)))
    if late:
        scratch += [pltpu.VMEM((rows, width), jnp.bfloat16), pltpu.SemaphoreType.DMA]
    kernel = functools.partial(
        side_kernel, label=label, raw_other=raw_other, has_sum=so_far is not None, finish=finish,
        written=written, late=late, step=step, chunk=chunk,
    )
    return pl.pallas_call(
        kernel,
        in_specs=specs,
        out_specs=ANYWHERE if written else IN_VMEM,
        out_shape=jax.ShapeDtypeStruct((rows, width), jnp.float32),
        scratch_shapes=scratch,
        input_output_aliases={sum_at: 0} if so_far is not None and not written else {},
        compiler_params=pltpu.CompilerParams(vmem_limit_bytes=VMEM_LIMIT),
        cost_estimate=pl.CostEstimate(
            flops=rows * width, bytes_accessed=rows * width, transcendentals=0
        ),
        name=name,
    )(*args)


def local(
    photo_vectors_raw, sentence_vectors_raw, companion_index, exponent_of_sharpness, affinity_offset
):
    exponent, offset = exponent_of_sharpness[0], affinity_offset[0]
    scalars = jnp.stack(
        [-LOG2E * jnp.exp(exponent), -LOG2E * offset, jnp.exp(-exponent), -LOG2E * exponent]
    )
    rows = photo_vectors_raw.shape[0]

    text_far = swapped(sentence_vectors_raw, 1)
    text_near = swapped(sentence_vectors_raw, 0)
    image_unit, image_norm, text_unit, text_norm, *parts = prepare(
        photo_vectors_raw, sentence_vectors_raw
    )
    text_sum = one_side(scalars, text_unit, image_unit, companion_index, "row", name="text_own")
    text_sum, near_part, image_unit = lax.optimization_barrier((text_sum, parts[0], image_unit))
    near_head = swapped(near_part, 0)
    image_sum = one_side(
        scalars, image_unit, text_unit, companion_index.reshape(rows, 1), "column", name="image_own"
    )
    image_sum, far_part = lax.optimization_barrier((image_sum, parts[2]))
    far_head = swapped(far_part, 1)
    image_sum = one_side(
        scalars, image_unit, text_near, raw_other=True, so_far=image_sum, name="image_near"
    )
    image_sum, text_sum, near_part, far_part = lax.optimization_barrier(
        (image_sum, text_sum, parts[1], parts[3])
    )
    near_tail = swapped(near_part, 0)
    far_tail = swapped(far_part, 1)
    text_sum = one_side(scalars, text_unit, near_head, so_far=text_sum, name="text_near_head")
    image_sum, text_sum = lax.optimization_barrier((image_sum, text_sum))
    image_grad = one_side(
        scalars, image_unit, text_far, raw_other=True, so_far=image_sum, finish="whole",
        rows_of=(photo_vectors_raw, image_norm), written=True, late=True, name="image_far",
    )
    image_grad, text_sum = lax.optimization_barrier((image_grad, text_sum))
    own_text = (sentence_vectors_raw, text_norm)
    text_sum = one_side(scalars, text_unit, near_tail, so_far=text_sum, name="text_near_tail")
    text_grad = one_side(
        scalars, text_unit, far_head, so_far=text_sum, finish="whole", rows_of=own_text,
        name="text_far_head",
    )
    text_grad = one_side(
        scalars, text_unit, far_tail, so_far=text_grad, finish="more", rows_of=own_text,
        written=True, name="text_far_tail",
    )
    return (image_grad, text_grad)


def solution(mesh):
    placed = (P(AXES, None), P(AXES, None), P(AXES, None), P(), P())
    return jax.shard_map(
        local, mesh=mesh, in_specs=placed, out_specs=(P(AXES, None), P(AXES, None)), check_vma=False
    )
```

```python
import functools

import jax
import jax.numpy as jnp
from jax import lax
from jax.experimental import pallas as pl
from jax.experimental.pallas import tpu as pltpu
from jax.sharding import PartitionSpec as P

AXES = ("grp", "dp")
LOG2E = 1.4426950408889634
VMEM_LIMIT = 24 * 2**20
NEAR_LAST, FAR_LAST = 384, 256
IN_VMEM = pl.BlockSpec(memory_space=pltpu.VMEM)
ANYWHERE = pl.BlockSpec(memory_space=pl.ANY)
IN_SMEM = pl.BlockSpec(memory_space=pltpu.SMEM)


def swapped(x, parity):
    devices = lax.axis_size(AXES)
    pairs = []
    for k in range(parity, devices, 2):
        after = (k + 1) % devices
        pairs += [(k, after), (after, k)]
    return lax.ppermute(x, AXES, pairs)


def unit_rows(raw):
    values = raw.astype(jnp.float32)
    norm = lax.rsqrt(jnp.sum(values * values, -1, keepdims=True) + 1e-06)
    return values * norm, norm


def prepare_kernel(image, text, *outs):
    image_out, image_norm, text_out, text_norm, *parts = outs
    rows, step = image.shape[0], 128
    for r in range(0, rows, step):
        at = slice(r, r + step)
        unit, image_norm[at, :] = unit_rows(image[at, :])
        unit = unit.astype(jnp.bfloat16)
        image_out[at, :] = unit
        for head, tail in (parts[:2], parts[2:]):
            count = head.shape[0]
            if r < count:
                head[at, :] = unit
            else:
                tail[r - count : r - count + step, :] = unit
        unit, text_norm[at, :] = unit_rows(text[at, :])
        text_out[at, :] = unit.astype(jnp.bfloat16)


def prepare(image, text):
    rows, width = image.shape
    unit = jax.ShapeDtypeStruct((rows, width), jnp.bfloat16)
    norm = jax.ShapeDtypeStruct((rows, 1), jnp.float32)
    parts = []
    for last in (NEAR_LAST, FAR_LAST):
        parts.append(jax.ShapeDtypeStruct((rows - last, width), jnp.bfloat16))
        parts.append(jax.ShapeDtypeStruct((last, width), jnp.bfloat16))
    return pl.pallas_call(
        prepare_kernel,
        in_specs=[IN_VMEM, IN_VMEM],
        out_specs=[IN_VMEM] * 8,
        out_shape=[unit, norm, unit, norm] + parts,
        compiler_params=pltpu.CompilerParams(vmem_limit_bytes=VMEM_LIMIT),
        cost_estimate=pl.CostEstimate(
            flops=8 * rows * width, bytes_accessed=8 * rows * width, transcendentals=2 * rows
        ),
        name="prepare",
    )(image, text)


def side_kernel(*refs, label, raw_other, has_sum, finish, written, late, beside, step, chunk):
    refs = list(refs)
    scalars, own_ref, other_ref = refs[:3]
    refs = refs[3:]
    pair_ref = refs.pop(0) if label else None
    sum_ref = refs.pop(0) if has_sum else None
    raw_ref, norm_ref = (refs.pop(0), refs.pop(0)) if finish else (None, None)
    if beside:
        del refs[:2]
    out_ref = refs.pop(0)
    rows, count = own_ref.shape[0], other_ref.shape[0]
    if raw_other:
        unit_ref = refs.pop(0)
        for r in range(0, count, 256):
            unit, _ = unit_rows(other_ref[r : r + 256, :])
            unit_ref[r : r + 256, :] = unit.astype(jnp.bfloat16)
    else:
        unit_ref = other_ref
    if written:
        grad_ref, sem = refs[:2]
    if late:
        late_ref, late_sem = refs[2:]
        fetch = pltpu.make_async_copy(raw_ref, late_ref, late_sem)
        fetch.start()
        raw_ref = late_ref
    slope, shift, floor, log_floor = (scalars[i] for i in range(4))

    def scores(r):
        own = own_ref[r : r + step, :]
        return [
            lax.dot_general(
                own,
                unit_ref[c : c + chunk, :],
                (((1,), (1,)), ((), ())),
                preferred_element_type=jnp.float32,
            )
            for c in range(0, count, chunk)
        ]

    def grad_tile(r, c, scores):
        power = slope * scores + shift
        if not label:
            tile = pltpu.reciprocal(floor + jnp.exp2(power + log_floor), approx=True)
        else:
            if label == "row":
                row_id = r + lax.broadcasted_iota(jnp.int32, (step, chunk), 0)
                match = row_id == pair_ref[:, c : c + chunk]
            else:
                column_id = c + lax.broadcasted_iota(jnp.int32, (step, chunk), 1)
                match = pair_ref[r : r + step, :] == column_id
            sign = jnp.where(match, -1.0, 1.0)
            tile = sign * pltpu.reciprocal(
                floor + jnp.exp2(sign * power + log_floor), approx=True
            )
        return tile.astype(jnp.bfloat16)

    coming = scores(0)
    for r in range(0, rows, step):
        at = slice(r, r + step)
        now, coming = coming, scores(r + step) if r + step < rows else None
        tiles = [grad_tile(r, i * chunk, part) for i, part in enumerate(now)]
        tile = tiles[0] if len(tiles) == 1 else jnp.concatenate(tiles, 1)
        total = jnp.dot(tile, unit_ref[...], preferred_element_type=jnp.float32)
        if late and r == 0:
            fetch.wait()
        if finish == "more":
            along = sum(
                jnp.sum(piece.astype(jnp.float32) * part, -1, keepdims=True)
                for piece, part in zip(tiles, now)
            )
            norm = norm_ref[at, :]
            raw = raw_ref[at, :].astype(jnp.float32)
            total = sum_ref[at, :] + norm * total - (norm * norm * along) * raw
        elif has_sum:
            total = total + sum_ref[at, :]
        if finish == "whole":
            norm = norm_ref[at, :]
            unit = raw_ref[at, :].astype(jnp.float32) * norm
            total = norm * (total - unit * jnp.sum(unit * total, -1, keepdims=True))
        if written:
            grad_ref[at, :] = total
            pltpu.make_async_copy(grad_ref.at[at], out_ref.at[at], sem.at[r // step]).start()
        else:
            out_ref[at, :] = total
    if written:
        for r in range(0, rows, step):
            at = slice(r, r + step)
            pltpu.make_async_copy(grad_ref.at[at], out_ref.at[at], sem.at[r // step]).wait()


def one_side(
    scalars, own, other, pair=None, label=None, raw_other=False, so_far=None, finish=None, rows_of=(),
    written=False, late=False, beside=None, step=256, chunk=256, name="side",
):
    rows, width = own.shape
    count = other.shape[0]
    chunk = chunk if count % chunk == 0 else count // 2
    args = [scalars, own, other]
    if label:
        args.append(pair)
    if so_far is not None:
        args.append(so_far)
    sum_at = len(args) - 1
    specs = [IN_SMEM] + [IN_VMEM] * sum_at
    if finish:
        args += list(rows_of)
        specs += [ANYWHERE if late else IN_VMEM, IN_VMEM]
    scratch = []
    if raw_other:
        scratch.append(pltpu.VMEM((count, width), jnp.bfloat16))
    if written:
        scratch.append(pltpu.VMEM((rows, width), jnp.float32))
        scratch.append(pltpu.SemaphoreType.DMA((rows // step,)))
    if late:
        scratch += [pltpu.VMEM((rows, width), jnp.bfloat16), pltpu.SemaphoreType.DMA]
    result = jax.ShapeDtypeStruct((rows, width), jnp.float32)
    place = ANYWHERE if written else IN_VMEM
    aliases = {sum_at: 0} if so_far is not None and not written else {}
    if beside is not None:
        args.append(beside)
        specs.append(ANYWHERE)
        result, place = [result, result], [ANYWHERE, place]
        aliases = {len(args) - 1: 0}
    kernel = functools.partial(
        side_kernel, label=label, raw_other=raw_other, has_sum=so_far is not None, finish=finish,
        written=written, late=late, beside=beside is not None, step=step, chunk=chunk,
    )
    return pl.pallas_call(
        kernel,
        in_specs=specs,
        out_specs=place,
        out_shape=result,
        scratch_shapes=scratch,
        input_output_aliases=aliases,
        compiler_params=pltpu.CompilerParams(vmem_limit_bytes=VMEM_LIMIT),
        cost_estimate=pl.CostEstimate(
            flops=rows * width, bytes_accessed=rows * width, transcendentals=0
        ),
        name=name,
    )(*args)


def local(
    photo_vectors_raw, sentence_vectors_raw, companion_index, exponent_of_sharpness, affinity_offset
):
    exponent, offset = exponent_of_sharpness[0], affinity_offset[0]
    scalars = jnp.stack(
        [-LOG2E * jnp.exp(exponent), -LOG2E * offset, jnp.exp(-exponent), -LOG2E * exponent]
    )
    rows = photo_vectors_raw.shape[0]

    text_far = swapped(sentence_vectors_raw, 1)
    text_near = swapped(sentence_vectors_raw, 0)
    image_unit, image_norm, text_unit, text_norm, *parts = prepare(
        photo_vectors_raw, sentence_vectors_raw
    )
    text_sum = one_side(scalars, text_unit, image_unit, companion_index, "row", name="text_own")
    text_sum, near_part, image_unit = lax.optimization_barrier((text_sum, parts[0], image_unit))
    near_head = swapped(near_part, 0)
    image_sum = one_side(
        scalars, image_unit, text_unit, companion_index.reshape(rows, 1), "column", name="image_own"
    )
    image_sum, far_part = lax.optimization_barrier((image_sum, parts[2]))
    far_head = swapped(far_part, 1)
    image_sum = one_side(
        scalars, image_unit, text_near, raw_other=True, so_far=image_sum, name="image_near"
    )
    image_sum, text_sum, near_part, far_part = lax.optimization_barrier(
        (image_sum, text_sum, parts[1], parts[3])
    )
    near_tail = swapped(near_part, 0)
    far_tail = swapped(far_part, 1)
    text_sum = one_side(scalars, text_unit, near_head, so_far=text_sum, name="text_near_head")
    image_sum, text_sum = lax.optimization_barrier((image_sum, text_sum))
    image_grad = one_side(
        scalars, image_unit, text_far, raw_other=True, so_far=image_sum, finish="whole",
        rows_of=(photo_vectors_raw, image_norm), written=True, late=True, name="image_far",
    )
    image_grad, text_sum = lax.optimization_barrier((image_grad, text_sum))
    own_text = (sentence_vectors_raw, text_norm)
    text_sum = one_side(scalars, text_unit, near_tail, so_far=text_sum, name="text_near_tail")
    text_grad = one_side(
        scalars, text_unit, far_head, so_far=text_sum, finish="whole", rows_of=own_text,
        name="text_far_head",
    )
    image_grad, text_grad = one_side(
        scalars, text_unit, far_tail, so_far=text_grad, finish="more", rows_of=own_text,
        written=True, beside=image_grad, name="text_far_tail",
    )
    return (image_grad, text_grad)


def solution(mesh):
    placed = (P(AXES, None), P(AXES, None), P(AXES, None), P(), P())
    return jax.shard_map(
        local, mesh=mesh, in_specs=placed, out_specs=(P(AXES, None), P(AXES, None)), check_vma=False
    )
```

```python
import functools

import jax
import jax.numpy as jnp
from jax import lax
from jax.experimental import pallas as pl
from jax.experimental.pallas import tpu as pltpu
from jax.sharding import PartitionSpec as P

AXES = ("grp", "dp")
LOG2E = 1.4426950408889634
VMEM_LIMIT = 24 * 2**20
NEAR_LAST, FAR_LAST = 384, 256
IN_VMEM = pl.BlockSpec(memory_space=pltpu.VMEM)
ANYWHERE = pl.BlockSpec(memory_space=pl.ANY)
IN_SMEM = pl.BlockSpec(memory_space=pltpu.SMEM)


def swapped(x, parity):
    devices = lax.axis_size(AXES)
    pairs = []
    for k in range(parity, devices, 2):
        after = (k + 1) % devices
        pairs += [(k, after), (after, k)]
    return lax.ppermute(x, AXES, pairs)


def unit_rows(raw):
    values = raw.astype(jnp.float32)
    norm = lax.rsqrt(jnp.sum(values * values, -1, keepdims=True) + 1e-06)
    return values * norm, norm


def prepare_kernel(image, text, *outs):
    image_out, image_norm, text_out, text_norm, *parts = outs
    rows, step = image.shape[0], 128
    for r in range(0, rows, step):
        at = slice(r, r + step)
        unit, image_norm[at, :] = unit_rows(image[at, :])
        unit = unit.astype(jnp.bfloat16)
        image_out[at, :] = unit
        for head, tail in (parts[:2], parts[2:]):
            count = head.shape[0]
            if r < count:
                head[at, :] = unit
            else:
                tail[r - count : r - count + step, :] = unit
        unit, text_norm[at, :] = unit_rows(text[at, :])
        text_out[at, :] = unit.astype(jnp.bfloat16)


def prepare(image, text):
    rows, width = image.shape
    unit = jax.ShapeDtypeStruct((rows, width), jnp.bfloat16)
    norm = jax.ShapeDtypeStruct((rows, 1), jnp.float32)
    parts = []
    for last in (NEAR_LAST, FAR_LAST):
        parts.append(jax.ShapeDtypeStruct((rows - last, width), jnp.bfloat16))
        parts.append(jax.ShapeDtypeStruct((last, width), jnp.bfloat16))
    return pl.pallas_call(
        prepare_kernel,
        in_specs=[IN_VMEM, IN_VMEM],
        out_specs=[IN_VMEM] * 8,
        out_shape=[unit, norm, unit, norm] + parts,
        compiler_params=pltpu.CompilerParams(vmem_limit_bytes=VMEM_LIMIT),
        cost_estimate=pl.CostEstimate(
            flops=8 * rows * width, bytes_accessed=8 * rows * width, transcendentals=2 * rows
        ),
        name="prepare",
    )(image, text)


def side_kernel(*refs, label, raw_other, has_sum, finish, written, beside, step, chunk):
    refs = list(refs)
    scalars, own_ref, other_ref = refs[:3]
    refs = refs[3:]
    pair_ref = refs.pop(0) if label else None
    sum_ref = refs.pop(0) if has_sum else None
    raw_ref, norm_ref = (refs.pop(0), refs.pop(0)) if finish else (None, None)
    if beside:
        del refs[:2]
    out_ref = refs.pop(0)
    rows, count = own_ref.shape[0], other_ref.shape[0]
    if raw_other:
        unit_ref = refs.pop(0)
        for r in range(0, count, 256):
            unit, _ = unit_rows(other_ref[r : r + 256, :])
            unit_ref[r : r + 256, :] = unit.astype(jnp.bfloat16)
    else:
        unit_ref = other_ref
    if written:
        grad_ref, sem = refs
    slope, shift, floor, log_floor = (scalars[i] for i in range(4))

    def scores(r):
        own = own_ref[r : r + step, :]
        return [
            lax.dot_general(
                own,
                unit_ref[c : c + chunk, :],
                (((1,), (1,)), ((), ())),
                preferred_element_type=jnp.float32,
            )
            for c in range(0, count, chunk)
        ]

    def grad_tile(r, c, scores):
        power = slope * scores + shift
        if not label:
            tile = pltpu.reciprocal(floor + jnp.exp2(power + log_floor), approx=True)
        else:
            if label == "row":
                row_id = r + lax.broadcasted_iota(jnp.int32, (step, chunk), 0)
                match = row_id == pair_ref[:, c : c + chunk]
            else:
                column_id = c + lax.broadcasted_iota(jnp.int32, (step, chunk), 1)
                match = pair_ref[r : r + step, :] == column_id
            sign = jnp.where(match, -1.0, 1.0)
            tile = sign * pltpu.reciprocal(
                floor + jnp.exp2(sign * power + log_floor), approx=True
            )
        return tile.astype(jnp.bfloat16)

    coming = scores(0)
    for r in range(0, rows, step):
        at = slice(r, r + step)
        now, coming = coming, scores(r + step) if r + step < rows else None
        tiles = [grad_tile(r, i * chunk, part) for i, part in enumerate(now)]
        tile = tiles[0] if len(tiles) == 1 else jnp.concatenate(tiles, 1)
        total = jnp.dot(tile, unit_ref[...], preferred_element_type=jnp.float32)
        if finish == "more":
            along = sum(
                jnp.sum(piece.astype(jnp.float32) * part, -1, keepdims=True)
                for piece, part in zip(tiles, now)
            )
            norm = norm_ref[at, :]
            raw = raw_ref[at, :].astype(jnp.float32)
            total = sum_ref[at, :] + norm * total - (norm * norm * along) * raw
        elif has_sum:
            total = total + sum_ref[at, :]
        if finish == "whole":
            norm = norm_ref[at, :]
            unit = raw_ref[at, :].astype(jnp.float32) * norm
            total = norm * (total - unit * jnp.sum(unit * total, -1, keepdims=True))
        if written:
            grad_ref[at, :] = total
            pltpu.make_async_copy(grad_ref.at[at], out_ref.at[at], sem.at[r // step]).start()
        else:
            out_ref[at, :] = total
    if written:
        for r in range(0, rows, step):
            at = slice(r, r + step)
            pltpu.make_async_copy(grad_ref.at[at], out_ref.at[at], sem.at[r // step]).wait()


def one_side(
    scalars, own, other, pair=None, label=None, raw_other=False, so_far=None, finish=None, rows_of=(),
    written=False, beside=None, step=256, chunk=256, name="side",
):
    rows, width = own.shape
    count = other.shape[0]
    chunk = chunk if count % chunk == 0 else count
    args = [scalars, own, other]
    if label:
        args.append(pair)
    if so_far is not None:
        args.append(so_far)
    sum_at = len(args) - 1
    specs = [IN_SMEM] + [IN_VMEM] * sum_at
    if finish:
        args += list(rows_of)
        specs += [IN_VMEM, IN_VMEM]
    scratch = []
    if raw_other:
        scratch.append(pltpu.VMEM((count, width), jnp.bfloat16))
    if written:
        scratch.append(pltpu.VMEM((rows, width), jnp.float32))
        scratch.append(pltpu.SemaphoreType.DMA((rows // step,)))
    result = jax.ShapeDtypeStruct((rows, width), jnp.float32)
    place = ANYWHERE if written else IN_VMEM
    aliases = {sum_at: 0} if so_far is not None and not written else {}
    if beside is not None:
        args.append(beside)
        specs.append(ANYWHERE)
        result, place = [result, result], [ANYWHERE, place]
        aliases = {len(args) - 1: 0}
    kernel = functools.partial(
        side_kernel, label=label, raw_other=raw_other, has_sum=so_far is not None, finish=finish,
        written=written, beside=beside is not None, step=step, chunk=chunk,
    )
    return pl.pallas_call(
        kernel,
        in_specs=specs,
        out_specs=place,
        out_shape=result,
        scratch_shapes=scratch,
        input_output_aliases=aliases,
        compiler_params=pltpu.CompilerParams(vmem_limit_bytes=VMEM_LIMIT),
        cost_estimate=pl.CostEstimate(
            flops=rows * width, bytes_accessed=rows * width, transcendentals=0
        ),
        name=name,
    )(*args)


def local(
    photo_vectors_raw, sentence_vectors_raw, companion_index, exponent_of_sharpness, affinity_offset
):
    exponent, offset = exponent_of_sharpness[0], affinity_offset[0]
    scalars = jnp.stack(
        [-LOG2E * jnp.exp(exponent), -LOG2E * offset, jnp.exp(-exponent), -LOG2E * exponent]
    )
    rows = photo_vectors_raw.shape[0]

    text_far = swapped(sentence_vectors_raw, 1)
    text_near = swapped(sentence_vectors_raw, 0)
    image_unit, image_norm, text_unit, text_norm, *parts = prepare(
        photo_vectors_raw, sentence_vectors_raw
    )
    text_sum = one_side(scalars, text_unit, image_unit, companion_index, "row", name="text_own")
    text_sum, near_part, image_unit = lax.optimization_barrier((text_sum, parts[0], image_unit))
    near_head = swapped(near_part, 0)
    image_sum = one_side(
        scalars, image_unit, text_unit, companion_index.reshape(rows, 1), "column", name="image_own"
    )
    image_sum, far_part = lax.optimization_barrier((image_sum, parts[2]))
    far_head = swapped(far_part, 1)
    image_sum = one_side(
        scalars, image_unit, text_near, raw_other=True, so_far=image_sum, name="image_near"
    )
    image_sum, text_sum, near_part, far_part = lax.optimization_barrier(
        (image_sum, text_sum, parts[1], parts[3])
    )
    near_tail = swapped(near_part, 0)
    far_tail = swapped(far_part, 1)
    text_sum = one_side(scalars, text_unit, near_head, so_far=text_sum, name="text_near_head")
    image_sum, text_sum = lax.optimization_barrier((image_sum, text_sum))
    image_grad = one_side(
        scalars, image_unit, text_far, raw_other=True, so_far=image_sum, finish="whole",
        rows_of=(photo_vectors_raw, image_norm), written=True, name="image_far",
    )
    image_grad, text_sum = lax.optimization_barrier((image_grad, text_sum))
    own_text = (sentence_vectors_raw, text_norm)
    text_sum = one_side(scalars, text_unit, near_tail, so_far=text_sum, name="text_near_tail")
    text_grad = one_side(
        scalars, text_unit, far_head, so_far=text_sum, finish="whole", rows_of=own_text,
        name="text_far_head",
    )
    image_grad, text_grad = one_side(
        scalars, text_unit, far_tail, so_far=text_grad, finish="more", rows_of=own_text,
        written=True, beside=image_grad, name="text_far_tail",
    )
    return (image_grad, text_grad)


def solution(mesh):
    placed = (P(AXES, None), P(AXES, None), P(AXES, None), P(), P())
    return jax.shard_map(
        local, mesh=mesh, in_specs=placed, out_specs=(P(AXES, None), P(AXES, None)), check_vma=False
    )
```
